32 devices in a mesh: dp: 8 (over z, y), tensor: 4 (over x, core).
Axes of the slice: x: 2, y: 2, z: 4, core: 2. Of those that a mesh axis runs over, the one named last changes fastest.
Arguments:
- hidden: bfloat16 [2, 512, 8192], P(None, 'dp', 'tensor'), may hold values from -6 to 6
- query_weight: bfloat16 [8192, 4096], P('tensor'), may hold values from -0.0625 to 0.0625
- key_weight: bfloat16 [8192, 512], P('tensor'), may hold values from -0.0625 to 0.0625
- value_weight: bfloat16 [8192, 512], P('tensor'), may hold values from -0.0625 to 0.0625
- adapter_down_weight: bfloat16 [8, 8192, 192], P('dp', 'tensor'), may hold values from -0.0625 to 0.0625
- adapter_up_query: bfloat16 [8, 64, 4096], P('dp', None, 'tensor'), may hold values from -0.75 to 0.75
- adapter_up_key_value: bfloat16 [8, 2, 64, 512], P('dp', None, None, 'tensor'), may hold values from -0.75 to 0.75
- cached_keys: bfloat16 [512, 96, 512], P('dp', None, 'tensor'), may hold values from -136 to 136
- cached_values: bfloat16 [512, 96, 512], P('dp', None, 'tensor'), may hold values from -6 to 6
- adapter_index: int32 [512, 1], P('dp'), may hold values from 0 to 7; in each aligned block of 64 rows (0 to 63, 64 to 127, ...) at most 16 rows name the same one
- cache_length: int32 [512], P('dp'), may hold values from 1 to 96, as said below
Outputs:
- attended: bfloat16 [2, 512, 4096], P(None, 'dp', 'tensor')
The draws below stay inside these ranges and needn't reach their ends.
Inputs may be any that keep to these rules, and one draw needn't show every extreme that they name: `adapter_index`: among the 64 requests of one device (aligned blocks of rows) no adapter is named more than 16 times, a bound that some block reaches. `cache_length`: one request of every device has a full cache of 96 positions.
All inputs are finite; a program needn't handle non-finite values.
Results may differ from the reference program's by a relative error of at most 0.012.
The reference program's roundings to bfloat16 on the way (of `shrunk` and `weights`) count: a program that leaves them out, or rounds other values in their place, can miss the bound.
Values may be sent and summed in bfloat16 or wider, within the bound.
A program may use at most 128 MiB of HBM per device.

```python
import math
import jax
import jax.numpy as jnp
import numpy as np
from jax import lax

MODEL_WIDTH = 8192
HEAD_WIDTH = 128
QUERY_HEADS = 32
KEY_HEADS = 4
ADAPTER_RANK = 64
NEW_POSITIONS = 2
REQ_DEV = 64
CACHE_SLOTS = 96
REQUEST_TOTAL = 512
ADAPTER_COUNT = 8
CAP = 16


def draw_cached_keys(key, part):
    key = jax.random.fold_in(key, 1)
    leading_step = jax.random.fold_in(key, 0)
    value_rows = jnp.clip(jax.random.normal(leading_step, (REQUEST_TOTAL, CACHE_SLOTS, KEY_HEADS * HEAD_WIDTH), jnp.float32), -6.0, 6.0)
    return value_rows.astype(jnp.bfloat16)


def draw_cache_length(key, part):
    key = jax.random.fold_in(key, 2)
    lengths = jax.random.randint(key, (REQUEST_TOTAL,), 1, CACHE_SLOTS + 1, dtype=jnp.int32)
    full_row = jnp.arange(REQUEST_TOTAL, dtype=jnp.int32) % REQ_DEV == 0
    return jnp.where(full_row, CACHE_SLOTS, lengths).astype(jnp.int32)


def steps_of(key, dims, cuts, least, largest):
    def one(position, blocks):
        heights = jax.random.uniform(jax.random.fold_in(jax.random.fold_in(key, 6), position), (blocks,), jnp.float32, least / len(cuts), largest / len(cuts))
        return jnp.repeat(jnp.exp(heights), dims[position] // blocks).reshape((-1,) + (1,) * (len(dims) - position - 1))

    factor_of = one(*cuts[0])
    for cut in cuts[1:]:
        factor_of = factor_of * one(*cut)
    return factor_of


def assign_block(key, own, number, rows, number_of, top, most, skew):
    ranking = jax.random.permutation(key, number_of)
    crowded, ordinary = load_shares(number_of, rows * top, most, skew, True), load_shares(number_of, rows * top, most, skew, False)
    places = jnp.arange(number_of)

    def named(sizes, offset_by):
        used = int((sizes > 0).sum())
        fixed = max(1, used // 4)
        passed = fixed + (places - fixed + offset_by * (used - fixed)) % max(1, number_of - fixed)
        return jnp.zeros((number_of,), jnp.int32).at[ranking[jnp.where(places < fixed, places, passed)]].set(jnp.asarray(sizes, jnp.int32))

    sizes = jnp.where(number % 4 == 0, named(crowded, number // 4), named(ordinary, number - number // 4 - 1))
    mixed = jax.random.permutation(jax.random.fold_in(own, 3), number_of)
    donor, taker = mixed[0:number_of // 2 * 2:2], mixed[1:number_of // 2 * 2:2]
    slack = jnp.minimum(sizes[donor] - 1, most - sizes[taker]) // 2
    slack = jnp.where((donor == ranking[0]) | (taker == ranking[0]) | (sizes[taker] == 0), 0, jnp.maximum(slack, 0))
    passed = jax.random.randint(jax.random.fold_in(own, 4), (number_of // 2,), 0, 1 << 20) % (slack + 1)
    sizes = sizes.at[donor].add(-passed).at[taker].add(passed)
    items = jnp.searchsorted(jnp.cumsum(sizes), jnp.arange(rows * top), side="right").astype(jnp.int32)
    grid = items.reshape(top, rows).T
    grid = grid[jax.random.permutation(jax.random.fold_in(own, 1), rows)]
    offset_by = jax.random.randint(jax.random.fold_in(own, 2), (rows, 1), 0, top)
    return jnp.take_along_axis(grid, (jnp.arange(top)[None, :] + offset_by) % top, axis=1)


def load_shares(number_of, total, reach, slope, full):
    weights = [(1 << 20) // math.isqrt(grade ** slope) + 1 for grade in range(1, number_of + 1)]
    largest = reach if full else min(reach, max(-(-total // number_of), total * weights[0] // sum(weights)))
    least = 1 if total - largest >= number_of - 1 else 0
    counts, spare = [largest] + [least] * (number_of - 1), total - largest - least * (number_of - 1)
    while spare > 0:
        candidates = [i for i in range(1, number_of) if counts[i] < largest] or [i for i in range(1, number_of) if counts[i] < reach]
        pool, left = sum([weights[i] for i in candidates]), spare
        for i in candidates:
            addition = min(reach - counts[i], max(1, left * weights[i] // pool), spare)
            counts[i] = counts[i] + addition
            spare = spare - addition
    return np.array(counts)


def centred(stream_key, dims, scale, most, cuts=(), kind=jnp.bfloat16):
    gain = steps_of(stream_key, dims, cuts, -0.22, 0.18) if cuts else 1.0
    array = jax.random.normal(stream_key, dims, jnp.float32) * scale * gain
    return jnp.minimum(jnp.maximum(array, -most), most).astype(kind)


def setup_inputs(seed: int = 0) -> dict:
    key_list = jax.random.split(jax.random.key(seed), 12)
    hidden = centred(key_list[0], (NEW_POSITIONS, REQUEST_TOTAL, MODEL_WIDTH), 1.0, 6.0, ((1, 8), (2, 4)))
    query_weight = centred(key_list[1], (MODEL_WIDTH, QUERY_HEADS * HEAD_WIDTH), MODEL_WIDTH ** -0.5, 0.0625, ((0, 4),))
    key_weight = centred(key_list[2], (MODEL_WIDTH, KEY_HEADS * HEAD_WIDTH), MODEL_WIDTH ** -0.5, 0.0625, ((0, 4),))
    value_weight = centred(key_list[3], (MODEL_WIDTH, KEY_HEADS * HEAD_WIDTH), MODEL_WIDTH ** -0.5, 0.0625, ((0, 4),))
    adapter_down_weight = centred(key_list[4], (ADAPTER_COUNT, MODEL_WIDTH, 3 * ADAPTER_RANK), MODEL_WIDTH ** -0.5, 0.0625, ((0, 8), (1, 4)))
    adapter_up_query = centred(key_list[5], (ADAPTER_COUNT, ADAPTER_RANK, QUERY_HEADS * HEAD_WIDTH), ADAPTER_RANK ** -0.5, 0.75, ((0, 8), (2, 4)))
    adapter_up_key_value = centred(key_list[6], (ADAPTER_COUNT, 2, ADAPTER_RANK, KEY_HEADS * HEAD_WIDTH), ADAPTER_RANK ** -0.5, 0.75, ((0, 8), (3, 4)))
    cached_keys = draw_cached_keys(jax.random.fold_in(key_list[11], 71), 0)
    cached_values = centred(key_list[8], (REQUEST_TOTAL, CACHE_SLOTS, KEY_HEADS * HEAD_WIDTH), 1.0, 6.0, ((0, 8), (2, 4)))
    adapter_index_keys = jax.random.split(jax.random.fold_in(key_list[9], 1), REQUEST_TOTAL // REQ_DEV)
    adapter_index_turns = jax.random.permutation(jax.random.fold_in(key_list[9], 3), REQUEST_TOTAL // REQ_DEV)
    adapter_index = jax.vmap(lambda own, number: assign_block(jax.random.fold_in(key_list[9], 2), own, number, REQ_DEV, ADAPTER_COUNT, 1, CAP, 2))(adapter_index_keys, adapter_index_turns).reshape((REQUEST_TOTAL, 1))
    cache_length = draw_cache_length(jax.random.fold_in(key_list[11], 71), 0)
    return dict(hidden=hidden, query_weight=query_weight, key_weight=key_weight, value_weight=value_weight, adapter_down_weight=adapter_down_weight, adapter_up_query=adapter_up_query, adapter_up_key_value=adapter_up_key_value, cached_keys=cached_keys, cached_values=cached_values, adapter_index=adapter_index, cache_length=cache_length)


adapter_scale = 0.5


def reference(hidden, query_weight, key_weight, value_weight, adapter_down_weight, adapter_up_query, adapter_up_key_value, cached_keys, cached_values, adapter_index, cache_length):
    flat_rows = hidden.reshape(NEW_POSITIONS * REQUEST_TOTAL, MODEL_WIDTH)
    plain_query = jnp.dot(flat_rows, query_weight, preferred_element_type=jnp.float32).reshape(NEW_POSITIONS, REQUEST_TOTAL, QUERY_HEADS * HEAD_WIDTH)
    plain_key = jnp.dot(flat_rows, key_weight, preferred_element_type=jnp.float32).reshape(NEW_POSITIONS, REQUEST_TOTAL, KEY_HEADS * HEAD_WIDTH)
    plain_value = jnp.dot(flat_rows, value_weight, preferred_element_type=jnp.float32).reshape(NEW_POSITIONS, REQUEST_TOTAL, KEY_HEADS * HEAD_WIDTH)
    chosen = adapter_index[:, 0].astype(jnp.int32)
    per_request = jnp.transpose(hidden, (1, 0, 2))

    def shrink_one(item):
        state_rows, selected_adapter = item
        return jnp.dot(state_rows, adapter_down_weight[selected_adapter], preferred_element_type=jnp.float32).astype(jnp.bfloat16)

    shrunk = lax.map(shrink_one, (per_request, chosen))

    def expand_one(item):
        input_rows, selected_adapter = item
        query_update = jnp.dot(input_rows[:, :ADAPTER_RANK], adapter_up_query[selected_adapter], preferred_element_type=jnp.float32).astype(jnp.bfloat16)
        key_update = jnp.dot(input_rows[:, ADAPTER_RANK:2 * ADAPTER_RANK], adapter_up_key_value[selected_adapter, 0], preferred_element_type=jnp.float32).astype(jnp.bfloat16)
        value_update = jnp.dot(input_rows[:, 2 * ADAPTER_RANK:], adapter_up_key_value[selected_adapter, 1], preferred_element_type=jnp.float32).astype(jnp.bfloat16)
        return query_update, key_update, value_update

    query_update, key_update, value_update = lax.map(expand_one, (shrunk, chosen))
    query_update = jnp.transpose(query_update, (1, 0, 2)).astype(jnp.float32)
    key_update = jnp.transpose(key_update, (1, 0, 2)).astype(jnp.float32)
    value_update = jnp.transpose(value_update, (1, 0, 2)).astype(jnp.float32)
    query_rows = (plain_query + adapter_scale * query_update).astype(jnp.bfloat16)
    appended_keys = (plain_key + adapter_scale * key_update).astype(jnp.bfloat16)
    appended_values = (plain_value + adapter_scale * value_update).astype(jnp.bfloat16)
    group_width = QUERY_HEADS // KEY_HEADS
    head_rows = query_rows.reshape(NEW_POSITIONS, REQUEST_TOTAL, KEY_HEADS, group_width, HEAD_WIDTH).astype(jnp.float32)
    fresh_keys = appended_keys.reshape(NEW_POSITIONS, REQUEST_TOTAL, KEY_HEADS, HEAD_WIDTH).astype(jnp.float32)
    fresh_values = appended_values.reshape(NEW_POSITIONS, REQUEST_TOTAL, KEY_HEADS, HEAD_WIDTH).astype(jnp.float32)
    prior_keys = cached_keys.reshape(REQUEST_TOTAL, CACHE_SLOTS, KEY_HEADS, HEAD_WIDTH).astype(jnp.float32)
    prior_values = cached_values.reshape(REQUEST_TOTAL, CACHE_SLOTS, KEY_HEADS, HEAD_WIDTH).astype(jnp.float32)
    factor = HEAD_WIDTH ** -0.5
    scores_old = jnp.einsum("srkgd,rckd->srkgc", head_rows, prior_keys) * factor
    scores_new = jnp.einsum("srkgd,trkd->srkgt", head_rows, fresh_keys) * factor
    valid_old = jnp.arange(CACHE_SLOTS, dtype=jnp.int32)[None, :] < cache_length.astype(jnp.int32)[:, None]
    valid_new = jnp.arange(NEW_POSITIONS, dtype=jnp.int32)[None, :] <= jnp.arange(NEW_POSITIONS, dtype=jnp.int32)[:, None]
    scores_old = jnp.where(valid_old[None, :, None, None, :], scores_old, -1e30)
    scores_new = jnp.where(valid_new[:, None, None, None, :], scores_new, -1e30)
    highest = jnp.maximum(jnp.max(scores_old, axis=-1), jnp.max(scores_new, axis=-1))
    exp_old = jnp.exp(scores_old - highest[..., None])
    exp_new = jnp.exp(scores_new - highest[..., None])
    denominator = jnp.sum(exp_old, axis=-1) + jnp.sum(exp_new, axis=-1)
    weight_old = (exp_old / denominator[..., None]).astype(jnp.bfloat16).astype(jnp.float32)
    weight_new = (exp_new / denominator[..., None]).astype(jnp.bfloat16).astype(jnp.float32)
    mixed = jnp.einsum("srkgc,rckd->srkgd", weight_old, prior_values) + jnp.einsum("srkgt,trkd->srkgd", weight_new, fresh_values)
    return mixed.reshape(NEW_POSITIONS, REQUEST_TOTAL, QUERY_HEADS * HEAD_WIDTH).astype(jnp.bfloat16)
```

```python
import jax
import jax.numpy as jnp
from jax import lax
from jax.sharding import PartitionSpec as P

HEAD_WIDTH = 128


adapter_scale = 0.5


def shards(
    hidden,
    query_weight,
    key_weight,
    value_weight,
    adapter_down_weight,
    adapter_up_query,
    adapter_up_key_value,
    cached_keys,
    cached_values,
    adapter_index,
    cache_length,
):
    step_count, request_count, part_width = hidden.shape
    row_count = step_count * request_count
    flat_rows = hidden.reshape(row_count, part_width)
    part_query = jnp.dot(flat_rows, query_weight, preferred_element_type=jnp.float32)
    part_key = jnp.dot(flat_rows, key_weight, preferred_element_type=jnp.float32)
    part_value = jnp.dot(flat_rows, value_weight, preferred_element_type=jnp.float32)
    plain_query, plain_key, plain_value = (
        lax.psum_scatter(part_query, "tensor", scatter_dimension=1, tiled=True),
        lax.psum_scatter(part_key, "tensor", scatter_dimension=1, tiled=True),
        lax.psum_scatter(part_value, "tensor", scatter_dimension=1, tiled=True),
    )
    query_width = plain_query.shape[1]
    kv_width = plain_key.shape[1]
    rank_span = adapter_up_query.shape[1]
    chosen = adapter_index[:, 0]
    owners = lax.axis_size("dp")
    capacity = max(2, 2 * request_count // owners)
    slot_rows = capacity * step_count
    onehot = (chosen[:, None] == jnp.arange(owners, dtype=jnp.int32)[None, :]).astype(jnp.int32)
    order = jnp.sum(onehot * (jnp.cumsum(onehot, axis=0) - 1), axis=1)
    target = chosen * capacity + order
    dispatch = (jnp.arange(owners * capacity, dtype=jnp.int32)[:, None] == target[None, :]).astype(
        jnp.bfloat16
    )
    outgoing = jnp.einsum(
        "mr,srd->msd", dispatch, hidden, preferred_element_type=jnp.float32
    ).astype(jnp.bfloat16)
    outgoing = outgoing.reshape(owners, slot_rows, part_width)
    arrived = lax.all_to_all(outgoing, "dp", 0, 0).reshape(owners * slot_rows, part_width)
    terms = jnp.dot(arrived, adapter_down_weight[0], preferred_element_type=jnp.float32)
    shrunk = lax.psum(terms, "tensor").astype(jnp.bfloat16)
    sum_query = jnp.dot(
        shrunk[:, :rank_span], adapter_up_query[0], preferred_element_type=jnp.float32
    )
    sum_key = jnp.dot(
        shrunk[:, rank_span : 2 * rank_span],
        adapter_up_key_value[0, 0],
        preferred_element_type=jnp.float32,
    )
    sum_value = jnp.dot(
        shrunk[:, 2 * rank_span :],
        adapter_up_key_value[0, 1],
        preferred_element_type=jnp.float32,
    )
    returned = jnp.concatenate(
        [
            sum_query.astype(jnp.bfloat16),
            sum_key.astype(jnp.bfloat16),
            sum_value.astype(jnp.bfloat16),
        ],
        axis=1,
    )
    returned = lax.all_to_all(returned.reshape(owners, slot_rows, -1), "dp", 0, 0)
    returned = returned.reshape(owners * capacity, step_count, query_width + 2 * kv_width)
    combined = jnp.einsum(
        "mr,msw->srw", dispatch, returned, preferred_element_type=jnp.float32
    ).astype(jnp.bfloat16)
    combined = combined.reshape(row_count, query_width + 2 * kv_width)
    query_update = combined[:, :query_width]
    key_update = combined[:, query_width : query_width + kv_width]
    value_update = combined[:, query_width + kv_width :]
    query_rows = (plain_query + adapter_scale * query_update.astype(jnp.float32)).astype(
        jnp.bfloat16
    )
    appended_keys = (plain_key + adapter_scale * key_update.astype(jnp.float32)).astype(
        jnp.bfloat16
    )
    appended_values = (plain_value + adapter_scale * value_update.astype(jnp.float32)).astype(
        jnp.bfloat16
    )
    local_heads = query_width // HEAD_WIDTH
    local_kv = kv_width // HEAD_WIDTH
    group_width = local_heads // local_kv
    cache_depth = cached_keys.shape[1]
    head_rows = query_rows.reshape(step_count, request_count, local_kv, group_width, HEAD_WIDTH)
    fresh_keys = appended_keys.reshape(step_count, request_count, local_kv, HEAD_WIDTH)
    fresh_values = appended_values.reshape(step_count, request_count, local_kv, HEAD_WIDTH)
    prior_keys = cached_keys.reshape(request_count, cache_depth, local_kv, HEAD_WIDTH)
    prior_values = cached_values.reshape(request_count, cache_depth, local_kv, HEAD_WIDTH)
    factor = HEAD_WIDTH ** (-0.5)
    scores_old = (
        jnp.einsum("srkgd,rckd->srkgc", head_rows, prior_keys, preferred_element_type=jnp.float32)
        * factor
    )
    scores_new = (
        jnp.einsum("srkgd,trkd->srkgt", head_rows, fresh_keys, preferred_element_type=jnp.float32)
        * factor
    )
    valid_old = jnp.arange(cache_depth, dtype=jnp.int32)[None, :] < cache_length[:, None]
    valid_new = (
        jnp.arange(step_count, dtype=jnp.int32)[None, :]
        <= jnp.arange(step_count, dtype=jnp.int32)[:, None]
    )
    scores_old = jnp.where(valid_old[None, :, None, None, :], scores_old, -1e30)
    scores_new = jnp.where(valid_new[:, None, None, None, :], scores_new, -1e30)
    highest = jnp.maximum(jnp.max(scores_old, axis=-1), jnp.max(scores_new, axis=-1))
    exp_old = jnp.exp(scores_old - highest[..., None])
    exp_new = jnp.exp(scores_new - highest[..., None])
    denominator = jnp.sum(exp_old, axis=-1) + jnp.sum(exp_new, axis=-1)
    weight_old = (exp_old / denominator[..., None]).astype(jnp.bfloat16)
    weight_new = (exp_new / denominator[..., None]).astype(jnp.bfloat16)
    mixed = jnp.einsum(
        "srkgc,rckd->srkgd", weight_old, prior_values, preferred_element_type=jnp.float32
    )
    mixed = mixed + jnp.einsum(
        "srkgt,trkd->srkgd", weight_new, fresh_values, preferred_element_type=jnp.float32
    )
    return mixed.reshape(step_count, request_count, query_width).astype(jnp.bfloat16)


def solution(mesh):
    return jax.shard_map(
        shards,
        mesh=mesh,
        in_specs=(
            P(None, "dp", "tensor"),
            P("tensor", None),
            P("tensor", None),
            P("tensor", None),
            P("dp", "tensor", None),
            P("dp", None, "tensor"),
            P("dp", None, None, "tensor"),
            P("dp", None, "tensor"),
            P("dp", None, "tensor"),
            P("dp", None),
            P("dp"),
        ),
        out_specs=P(None, "dp", "tensor"),
        check_vma=False,
    )
```

```python
import functools

import jax
import jax.numpy as jnp
from jax import lax
from jax.experimental import pallas as pl
from jax.experimental.pallas import tpu as pltpu
from jax.sharding import PartitionSpec as P

HEAD_WIDTH = 128
MESH = pl.DeviceIdType.MESH

adapter_scale = 0.5


def project_kernel(
    owners,
    hid_ref, disp_ref, back_ref, down_ref, up_ref, wq_ref, wk_ref, wv_ref,
    out_ref,
    wbuf, part, rs1, rs2, outgoing, arrived, terms, terms_in, sums, sums_in, delta, returned,
    w_sem, d_send, d_recv, r_send, r_recv, x_send, x_recv,
):
    me = lax.axis_index("dp")
    t = lax.axis_index("tensor")
    pair = t + 1 - 2 * (t % 2)
    across = (t + 2) % 4
    targets = {0: t, 1: pair, 2: across, 3: (pair + 2) % 4}
    order = (3, 2, 1, 0)
    width = part.shape[2]
    q_width = wq_ref.shape[1] // 4
    kv_width = wk_ref.shape[1] // 4

    def weight_copies(k):
        q_cols = pl.ds(pl.multiple_of(targets[k] * q_width, 128), q_width)
        kv_cols = pl.ds(pl.multiple_of(targets[k] * kv_width, 128), kv_width)
        return (
            pltpu.make_async_copy(
                wq_ref.at[:, q_cols], wbuf.at[k, :, pl.ds(0, q_width)], w_sem.at[k, 0]
            ),
            pltpu.make_async_copy(
                wk_ref.at[:, kv_cols], wbuf.at[k, :, pl.ds(q_width, kv_width)], w_sem.at[k, 1]
            ),
            pltpu.make_async_copy(
                wv_ref.at[:, kv_cols],
                wbuf.at[k, :, pl.ds(q_width + kv_width, kv_width)],
                w_sem.at[k, 2],
            ),
        )

    for k in order:
        for copy in weight_copies(k):
            copy.start()

    barrier = pltpu.get_barrier_semaphore()

    @pl.loop(1, owners)
    def _(i):
        pl.semaphore_signal(
            barrier, inc=1, device_id={"dp": (me + i) % owners}, device_id_type=MESH
        )

    for peer in (pair, across):
        pl.semaphore_signal(barrier, inc=1, device_id={"tensor": peer}, device_id_type=MESH)
    pl.semaphore_wait(barrier, owners + 1)

    def dispatch_copy(i):
        return pltpu.make_async_remote_copy(
            src_ref=outgoing.at[i],
            dst_ref=arrived.at[i],
            send_sem=d_send.at[i],
            recv_sem=d_recv.at[i],
            device_id={"dp": (me + i) % owners},
            device_id_type=MESH,
        )

    def return_copy(i):
        return pltpu.make_async_remote_copy(
            src_ref=delta.at[i],
            dst_ref=returned.at[i],
            send_sem=r_send.at[i],
            recv_sem=r_recv.at[i],
            device_id={"dp": (me + owners - i) % owners},
            device_id_type=MESH,
        )

    def tensor_copy(src, dst, number, peer):
        return pltpu.make_async_remote_copy(
            src_ref=src,
            dst_ref=dst,
            send_sem=x_send.at[number],
            recv_sem=x_recv.at[number],
            device_id={"tensor": peer},
            device_id_type=MESH,
        )

    def picked(i):
        return jnp.dot(
            disp_ref[i], hid_ref[...], preferred_element_type=jnp.float32
        ).astype(jnp.bfloat16)

    @pl.loop(1, owners)
    def _(i):
        outgoing[i] = picked(i)
        dispatch_copy(i).start()

    arrived[0] = picked(0)

    tile = 256

    def project(k):
        for copy in weight_copies(k):
            copy.wait()

        @pl.loop(0, width // tile)
        def _(c):
            cols = pl.ds(pl.multiple_of(c * tile, tile), tile)
            part[k, :, cols] = jnp.dot(
                hid_ref[...], wbuf[k, :, cols], preferred_element_type=jnp.float32
            )

    own_copy = tensor_copy(part.at[1], rs1.at[0], 0, pair)
    far_copy = tensor_copy(part.at[3], rs1.at[1], 1, pair)
    sum_copy = tensor_copy(part.at[2], rs2, 2, across)
    project(3)
    far_copy.start()
    project(2)
    far_copy.wait()
    part[2] = part[2] + rs1[1]
    sum_copy.start()
    project(1)
    own_copy.start()
    project(0)

    def shrink(i):
        terms[i] = jnp.dot(arrived[i], down_ref[...], preferred_element_type=jnp.float32)

    shrink(0)

    @pl.loop(1, owners)
    def _(i):
        dispatch_copy(i).wait()
        shrink(i)

    terms_copy = tensor_copy(terms, terms_in, 3, pair)
    terms_copy.start()
    terms_copy.wait()
    sums[...] = terms[...] + terms_in[...]
    sums_copy = tensor_copy(sums, sums_in, 4, across)
    sums_copy.start()
    sums_copy.wait()

    def expand(i):
        shrunk = (sums[i] + sums_in[i]).astype(jnp.bfloat16)
        return jnp.dot(
            shrunk, up_ref[...], preferred_element_type=jnp.float32
        ).astype(jnp.bfloat16)

    @pl.loop(1, owners)
    def _(i):
        delta[i] = expand(i)
        return_copy(i).start()

    returned[0] = expand(0)
    own_copy.wait()
    sum_copy.wait()
    part[0] = part[0] + rs1[0] + rs2[...]

    def combine(i):
        part[1] = part[1] + jnp.dot(
            back_ref[i], returned[i], preferred_element_type=jnp.float32
        )

    part[1] = jnp.zeros(part.shape[1:], jnp.float32)
    combine(0)

    @pl.loop(1, owners)
    def _(i):
        return_copy(i).wait()
        combine(i)

    out_ref[...] = (part[0] + adapter_scale * part[1]).astype(jnp.bfloat16)


def shards(
    hidden,
    query_weight,
    key_weight,
    value_weight,
    adapter_down_weight,
    adapter_up_query,
    adapter_up_key_value,
    cached_keys,
    cached_values,
    adapter_index,
    cache_length,
):
    step_count, request_count, part_width = hidden.shape
    row_count = step_count * request_count
    flat_rows = hidden.reshape(row_count, part_width)
    owners = lax.axis_size("dp")
    rank_span = adapter_up_query.shape[1]
    query_width = adapter_up_query.shape[2]
    kv_width = adapter_up_key_value.shape[3]
    width = query_width + 2 * kv_width
    rank_pad = -(-3 * rank_span // 128) * 128
    capacity = max(2, 2 * request_count // owners)
    slot_rows = capacity * step_count
    chosen = adapter_index[:, 0]
    places = jnp.arange(request_count, dtype=jnp.int32)
    earlier = (chosen[:, None] == chosen[None, :]) & (places[None, :] < places[:, None])
    order = jnp.sum(earlier.astype(jnp.int32), axis=1)
    offset = (chosen - lax.axis_index("dp") + owners) % owners
    steps = jnp.arange(step_count, dtype=jnp.int32)
    slot = (offset * slot_rows + order)[None, :] + capacity * steps[:, None]
    slot = slot.reshape(row_count)
    numbers = jnp.arange(owners * slot_rows, dtype=jnp.int32)
    dispatch = (numbers.reshape(owners, slot_rows, 1) == slot[None, None, :]).astype(jnp.bfloat16)
    back = (numbers.reshape(owners, 1, slot_rows) == slot[None, :, None]).astype(jnp.bfloat16)
    down = jnp.pad(adapter_down_weight[0], ((0, 0), (0, rank_pad - 3 * rank_span)))
    up = jnp.concatenate(
        [
            jnp.pad(adapter_up_query[0], ((0, rank_pad - rank_span), (0, 0))),
            jnp.pad(adapter_up_key_value[0, 0], ((rank_span, rank_pad - 2 * rank_span), (0, 0))),
            jnp.pad(
                adapter_up_key_value[0, 1], ((2 * rank_span, rank_pad - 3 * rank_span), (0, 0))
            ),
        ],
        axis=1,
    )
    f32, bf16 = jnp.float32, jnp.bfloat16
    vmem = pl.BlockSpec(memory_space=pltpu.VMEM)
    hbm = pl.BlockSpec(memory_space=pl.ANY)
    rows = pl.pallas_call(
        functools.partial(project_kernel, owners),
        out_shape=jax.ShapeDtypeStruct((row_count, width), bf16),
        in_specs=[vmem] * 5 + [hbm] * 3,
        out_specs=vmem,
        scratch_shapes=[
            pltpu.VMEM((4, part_width, width), bf16),
            pltpu.VMEM((4, row_count, width), f32),
            pltpu.VMEM((2, row_count, width), f32),
            pltpu.VMEM((row_count, width), f32),
            pltpu.VMEM((owners, slot_rows, part_width), bf16),
            pltpu.VMEM((owners, slot_rows, part_width), bf16),
            pltpu.VMEM((owners, slot_rows, rank_pad), f32),
            pltpu.VMEM((owners, slot_rows, rank_pad), f32),
            pltpu.VMEM((owners, slot_rows, rank_pad), f32),
            pltpu.VMEM((owners, slot_rows, rank_pad), f32),
            pltpu.VMEM((owners, slot_rows, width), bf16),
            pltpu.VMEM((owners, slot_rows, width), bf16),
            pltpu.SemaphoreType.DMA((4, 3)),
            pltpu.SemaphoreType.DMA((owners,)),
            pltpu.SemaphoreType.DMA((owners,)),
            pltpu.SemaphoreType.DMA((owners,)),
            pltpu.SemaphoreType.DMA((owners,)),
            pltpu.SemaphoreType.DMA((5,)),
            pltpu.SemaphoreType.DMA((5,)),
        ],
        compiler_params=pltpu.CompilerParams(
            collective_id=0, has_side_effects=True, vmem_limit_bytes=52 * 1024 * 1024
        ),
    )(flat_rows, dispatch, back, down, up, query_weight, key_weight, value_weight)
    query_rows = rows[:, :query_width]
    appended_keys = rows[:, query_width : query_width + kv_width]
    appended_values = rows[:, query_width + kv_width :]
    local_heads = query_width // HEAD_WIDTH
    local_kv = kv_width // HEAD_WIDTH
    group_width = local_heads // local_kv
    cache_depth = cached_keys.shape[1]
    head_rows = query_rows.reshape(step_count, request_count, local_kv, group_width, HEAD_WIDTH)
    fresh_keys = appended_keys.reshape(step_count, request_count, local_kv, HEAD_WIDTH)
    fresh_values = appended_values.reshape(step_count, request_count, local_kv, HEAD_WIDTH)
    prior_keys = cached_keys.reshape(request_count, cache_depth, local_kv, HEAD_WIDTH)
    prior_values = cached_values.reshape(request_count, cache_depth, local_kv, HEAD_WIDTH)
    factor = HEAD_WIDTH ** (-0.5)
    scores_old = (
        jnp.einsum("srkgd,rckd->srkgc", head_rows, prior_keys, preferred_element_type=jnp.float32)
        * factor
    )
    scores_new = (
        jnp.einsum("srkgd,trkd->srkgt", head_rows, fresh_keys, preferred_element_type=jnp.float32)
        * factor
    )
    valid_old = jnp.arange(cache_depth, dtype=jnp.int32)[None, :] < cache_length[:, None]
    valid_new = (
        jnp.arange(step_count, dtype=jnp.int32)[None, :]
        <= jnp.arange(step_count, dtype=jnp.int32)[:, None]
    )
    scores_old = jnp.where(valid_old[None, :, None, None, :], scores_old, -1e30)
    scores_new = jnp.where(valid_new[:, None, None, None, :], scores_new, -1e30)
    highest = jnp.maximum(jnp.max(scores_old, axis=-1), jnp.max(scores_new, axis=-1))
    exp_old = jnp.exp(scores_old - highest[..., None])
    exp_new = jnp.exp(scores_new - highest[..., None])
    denominator = jnp.sum(exp_old, axis=-1) + jnp.sum(exp_new, axis=-1)
    weight_old = (exp_old / denominator[..., None]).astype(jnp.bfloat16)
    weight_new = (exp_new / denominator[..., None]).astype(jnp.bfloat16)
    mixed = jnp.einsum(
        "srkgc,rckd->srkgd", weight_old, prior_values, preferred_element_type=jnp.float32
    )
    mixed = mixed + jnp.einsum(
        "srkgt,trkd->srkgd", weight_new, fresh_values, preferred_element_type=jnp.float32
    )
    return mixed.reshape(step_count, request_count, query_width).astype(jnp.bfloat16)


def solution(mesh):
    return jax.shard_map(
        shards,
        mesh=mesh,
        in_specs=(
            P(None, "dp", "tensor"),
            P("tensor", None),
            P("tensor", None),
            P("tensor", None),
            P("dp", "tensor", None),
            P("dp", None, "tensor"),
            P("dp", None, None, "tensor"),
            P("dp", None, "tensor"),
            P("dp", None, "tensor"),
            P("dp", None),
            P("dp"),
        ),
        out_specs=P(None, "dp", "tensor"),
        check_vma=False,
    )
```

```python
import functools

import jax
import jax.numpy as jnp
from jax import lax
from jax.experimental import pallas as pl
from jax.experimental.pallas import tpu as pltpu
from jax.sharding import PartitionSpec as P

HEAD_WIDTH = 128
MESH = pl.DeviceIdType.MESH

adapter_scale = 0.5


def project_kernel(
    owners,
    hid_ref, disp_ref, back_ref, down_ref, up_ref, wq_ref, wk_ref, wv_ref,
    out_ref,
    wbuf, part, rs1, rs2, outgoing, arrived, terms, terms_in, sums, sums_in, delta, returned,
    w_sem, d_send, d_recv, r_send, r_recv, x_send, x_recv,
):
    me = lax.axis_index("dp")
    t = lax.axis_index("tensor")
    pair = t + 1 - 2 * (t % 2)
    across = (t + 2) % 4
    targets = {0: t, 1: pair, 2: across, 3: (pair + 2) % 4}
    order = (3, 2, 1, 0)
    width = part.shape[2]
    rank = down_ref.shape[1]
    groups = back_ref.shape[0]
    members = owners // groups

    def partner(i):
        total, bit = 0, 1
        while bit < owners:
            total = total + ((me // bit + i // bit) % 2) * bit
            bit *= 2
        return total

    q_width = wq_ref.shape[1] // 4
    kv_width = wk_ref.shape[1] // 4

    def weight_copies(k):
        q_cols = pl.ds(pl.multiple_of(targets[k] * q_width, 128), q_width)
        kv_cols = pl.ds(pl.multiple_of(targets[k] * kv_width, 128), kv_width)
        return (
            pltpu.make_async_copy(
                wq_ref.at[:, q_cols], wbuf.at[k, :, pl.ds(0, q_width)], w_sem.at[k, 0]
            ),
            pltpu.make_async_copy(
                wk_ref.at[:, kv_cols], wbuf.at[k, :, pl.ds(q_width, kv_width)], w_sem.at[k, 1]
            ),
            pltpu.make_async_copy(
                wv_ref.at[:, kv_cols],
                wbuf.at[k, :, pl.ds(q_width + kv_width, kv_width)],
                w_sem.at[k, 2],
            ),
        )

    for k in order:
        for copy in weight_copies(k):
            copy.start()

    barrier = pltpu.get_barrier_semaphore()

    @pl.loop(1, owners)
    def _(i):
        pl.semaphore_signal(
            barrier, inc=1, device_id={"dp": partner(i)}, device_id_type=MESH
        )

    for peer in (pair, across):
        pl.semaphore_signal(barrier, inc=1, device_id={"tensor": peer}, device_id_type=MESH)
    pl.semaphore_wait(barrier, owners + 1)

    def dispatch_copy(i):
        return pltpu.make_async_remote_copy(
            src_ref=outgoing.at[i],
            dst_ref=arrived.at[i],
            send_sem=d_send.at[i],
            recv_sem=d_recv.at[i],
            device_id={"dp": partner(i)},
            device_id_type=MESH,
        )

    def return_copy(i):
        return pltpu.make_async_remote_copy(
            src_ref=delta.at[i],
            dst_ref=returned.at[i],
            send_sem=r_send.at[i],
            recv_sem=r_recv.at[i],
            device_id={"dp": partner(i)},
            device_id_type=MESH,
        )

    def tensor_copy(src, dst, number, peer):
        return pltpu.make_async_remote_copy(
            src_ref=src,
            dst_ref=dst,
            send_sem=x_send.at[number],
            recv_sem=x_recv.at[number],
            device_id={"tensor": peer},
            device_id_type=MESH,
        )

    def picked(i):
        return jnp.dot(
            disp_ref[i], hid_ref[...], preferred_element_type=jnp.float32
        ).astype(jnp.bfloat16)

    @pl.loop(1, owners)
    def _(i):
        outgoing[owners - i] = picked(owners - i)
        dispatch_copy(owners - i).start()

    arrived[0] = picked(0)

    tile = 256

    def project(k):
        for copy in weight_copies(k):
            copy.wait()

        @pl.loop(0, width // tile)
        def _(c):
            cols = pl.ds(pl.multiple_of(c * tile, tile), tile)
            part[k, :, cols] = jnp.dot(
                hid_ref[...], wbuf[k, :, cols], preferred_element_type=jnp.float32
            )

    own_copy = tensor_copy(part.at[1], rs1.at[0], 0, pair)
    far_copy = tensor_copy(part.at[3], rs1.at[1], 1, pair)
    sum_copy = tensor_copy(part.at[2], rs2, 2, across)
    project(3)
    far_copy.start()
    project(2)
    far_copy.wait()
    part[2] = part[2] + rs1[1]
    sum_copy.start()
    project(1)
    own_copy.start()
    project(0)

    own_copy.wait()
    part[0] = part[0] + rs1[0]
    terms[...] = jnp.zeros_like(terms)

    def pair_copy(i):
        return tensor_copy(terms.at[i], terms_in.at[i], 3 + i, pair)

    def across_copy(i):
        return tensor_copy(sums.at[i], sums_in.at[i], 3 + owners + i, across)

    def expand(i):
        shrunk = (sums[i] + sums_in[i])[:, :rank].astype(jnp.bfloat16)
        return jnp.dot(
            shrunk, up_ref[...], preferred_element_type=jnp.float32
        ).astype(jnp.bfloat16)

    @pl.loop(0, owners + 2)
    def _(i):
        @pl.when(i < owners)
        def _():
            @pl.when(i > 0)
            def _():
                dispatch_copy(i).wait()

            terms[i, :, pl.ds(0, rank)] = jnp.dot(
                arrived[i], down_ref[...], preferred_element_type=jnp.float32
            )
            pair_copy(i).start()

        @pl.when((i >= 1) & (i <= owners))
        def _():
            pair_copy(i - 1).wait()
            sums[i - 1] = terms[i - 1] + terms_in[i - 1]
            across_copy(i - 1).start()

        @pl.when(i >= 2)
        def _():
            across_copy(i - 2).wait()

            @pl.when(i == 2)
            def _():
                returned[0] = expand(0)

            @pl.when(i > 2)
            def _():
                delta[i - 2] = expand(i - 2)
                return_copy(i - 2).start()

    sum_copy.wait()
    part[0] = part[0] + rs2[...]
    part[1] = jnp.zeros(part.shape[1:], jnp.float32)

    @pl.loop(0, groups)
    def _(g):
        @pl.loop(0, members)
        def _(j):
            @pl.when(g * members + j > 0)
            def _():
                return_copy(g * members + j).wait()

        if members == 1:
            block = returned[g]
        else:
            block = returned[pl.ds(g * members, members)]
            block = block.reshape(members * block.shape[1], width)
        part[1] = part[1] + jnp.dot(back_ref[g], block, preferred_element_type=jnp.float32)

    out_ref[...] = (part[0] + adapter_scale * part[1]).astype(jnp.bfloat16)


def shards(
    hidden,
    query_weight,
    key_weight,
    value_weight,
    adapter_down_weight,
    adapter_up_query,
    adapter_up_key_value,
    cached_keys,
    cached_values,
    adapter_index,
    cache_length,
):
    step_count, request_count, part_width = hidden.shape
    row_count = step_count * request_count
    flat_rows = hidden.reshape(row_count, part_width)
    owners = lax.axis_size("dp")
    rank_span = adapter_up_query.shape[1]
    query_width = adapter_up_query.shape[2]
    kv_width = adapter_up_key_value.shape[3]
    width = query_width + 2 * kv_width
    rank_pad = -(-3 * rank_span // 128) * 128
    capacity = max(2, 2 * request_count // owners)
    slot_rows = capacity * step_count
    chosen = adapter_index[:, 0]
    places = jnp.arange(request_count, dtype=jnp.int32)
    earlier = (chosen[:, None] == chosen[None, :]) & (places[None, :] < places[:, None])
    order = jnp.sum(earlier.astype(jnp.int32), axis=1)
    offset = chosen ^ lax.axis_index("dp")
    steps = jnp.arange(step_count, dtype=jnp.int32)
    slot = (offset * slot_rows + order)[None, :] + capacity * steps[:, None]
    slot = slot.reshape(row_count)
    numbers = jnp.arange(owners * slot_rows, dtype=jnp.int32)
    dispatch = (numbers.reshape(owners, slot_rows, 1) == slot[None, None, :]).astype(jnp.bfloat16)
    groups = 2 if slot_rows % 16 == 0 and owners * slot_rows % 256 == 0 else owners
    back = (numbers.reshape(groups, 1, -1) == slot[None, :, None]).astype(jnp.bfloat16)
    down = adapter_down_weight[0]
    up = jnp.concatenate(
        [
            jnp.pad(adapter_up_query[0], ((0, 3 * rank_span - rank_span), (0, 0))),
            jnp.pad(adapter_up_key_value[0, 0], ((rank_span, 3 * rank_span - 2 * rank_span), (0, 0))),
            jnp.pad(
                adapter_up_key_value[0, 1], ((2 * rank_span, 0), (0, 0))
            ),
        ],
        axis=1,
    )
    f32, bf16 = jnp.float32, jnp.bfloat16
    vmem = pl.BlockSpec(memory_space=pltpu.VMEM)
    hbm = pl.BlockSpec(memory_space=pl.ANY)
    rows = pl.pallas_call(
        functools.partial(project_kernel, owners),
        out_shape=jax.ShapeDtypeStruct((row_count, width), bf16),
        in_specs=[vmem] * 5 + [hbm] * 3,
        out_specs=vmem,
        scratch_shapes=[
            pltpu.VMEM((4, part_width, width), bf16),
            pltpu.VMEM((4, row_count, width), f32),
            pltpu.VMEM((2, row_count, width), f32),
            pltpu.VMEM((row_count, width), f32),
            pltpu.VMEM((owners, slot_rows, part_width), bf16),
            pltpu.VMEM((owners, slot_rows, part_width), bf16),
            pltpu.VMEM((owners, slot_rows, rank_pad), f32),
            pltpu.VMEM((owners, slot_rows, rank_pad), f32),
            pltpu.VMEM((owners, slot_rows, rank_pad), f32),
            pltpu.VMEM((owners, slot_rows, rank_pad), f32),
            pltpu.VMEM((owners, slot_rows, width), bf16),
            pltpu.VMEM((owners, slot_rows, width), bf16),
            pltpu.SemaphoreType.DMA((4, 3)),
            pltpu.SemaphoreType.DMA((owners,)),
            pltpu.SemaphoreType.DMA((owners,)),
            pltpu.SemaphoreType.DMA((owners,)),
            pltpu.SemaphoreType.DMA((owners,)),
            pltpu.SemaphoreType.DMA((3 + 2 * owners,)),
            pltpu.SemaphoreType.DMA((3 + 2 * owners,)),
        ],
        compiler_params=pltpu.CompilerParams(
            collective_id=0, has_side_effects=True, vmem_limit_bytes=52 * 1024 * 1024
        ),
    )(flat_rows, dispatch, back, down, up, query_weight, key_weight, value_weight)
    query_rows = rows[:, :query_width]
    appended_keys = rows[:, query_width : query_width + kv_width]
    appended_values = rows[:, query_width + kv_width :]
    local_heads = query_width // HEAD_WIDTH
    local_kv = kv_width // HEAD_WIDTH
    group_width = local_heads // local_kv
    cache_depth = cached_keys.shape[1]
    head_rows = query_rows.reshape(step_count, request_count, local_kv, group_width, HEAD_WIDTH)
    fresh_keys = appended_keys.reshape(step_count, request_count, local_kv, HEAD_WIDTH)
    fresh_values = appended_values.reshape(step_count, request_count, local_kv, HEAD_WIDTH)
    prior_keys = cached_keys.reshape(request_count, cache_depth, local_kv, HEAD_WIDTH)
    prior_values = cached_values.reshape(request_count, cache_depth, local_kv, HEAD_WIDTH)
    factor = HEAD_WIDTH ** (-0.5)
    scores_old = (
        jnp.einsum("srkgd,rckd->srkgc", head_rows, prior_keys, preferred_element_type=jnp.float32)
        * factor
    )
    scores_new = (
        jnp.einsum("srkgd,trkd->srkgt", head_rows, fresh_keys, preferred_element_type=jnp.float32)
        * factor
    )
    valid_old = jnp.arange(cache_depth, dtype=jnp.int32)[None, :] < cache_length[:, None]
    valid_new = (
        jnp.arange(step_count, dtype=jnp.int32)[None, :]
        <= jnp.arange(step_count, dtype=jnp.int32)[:, None]
    )
    scores_old = jnp.where(valid_old[None, :, None, None, :], scores_old, -1e30)
    scores_new = jnp.where(valid_new[:, None, None, None, :], scores_new, -1e30)
    highest = jnp.maximum(jnp.max(scores_old, axis=-1), jnp.max(scores_new, axis=-1))
    exp_old = jnp.exp(scores_old - highest[..., None])
    exp_new = jnp.exp(scores_new - highest[..., None])
    denominator = jnp.sum(exp_old, axis=-1) + jnp.sum(exp_new, axis=-1)
    weight_old = (exp_old / denominator[..., None]).astype(jnp.bfloat16)
    weight_new = (exp_new / denominator[..., None]).astype(jnp.bfloat16)
    mixed = jnp.einsum(
        "srkgc,rckd->srkgd", weight_old, prior_values, preferred_element_type=jnp.float32
    )
    mixed = mixed + jnp.einsum(
        "srkgt,trkd->srkgd", weight_new, fresh_values, preferred_element_type=jnp.float32
    )
    return mixed.reshape(step_count, request_count, query_width).astype(jnp.bfloat16)


def solution(mesh):
    return jax.shard_map(
        shards,
        mesh=mesh,
        in_specs=(
            P(None, "dp", "tensor"),
            P("tensor", None),
            P("tensor", None),
            P("tensor", None),
            P("dp", "tensor", None),
            P("dp", None, "tensor"),
            P("dp", None, None, "tensor"),
            P("dp", None, "tensor"),
            P("dp", None, "tensor"),
            P("dp", None),
            P("dp"),
        ),
        out_specs=P(None, "dp", "tensor"),
        check_vma=False,
    )
```

```python
import functools

import jax
import jax.numpy as jnp
from jax import lax
from jax.experimental import pallas as pl
from jax.experimental.pallas import tpu as pltpu
from jax.sharding import PartitionSpec as P

HEAD_WIDTH = 128
MESH = pl.DeviceIdType.MESH

adapter_scale = 0.5


def project_kernel(
    owners,
    hid_ref, disp_ref, back_ref, down_ref, up_q_ref, up_kv_ref, wq_ref, wk_ref, wv_ref,
    out_ref,
    wbuf, part, rs1, rs2, outgoing, arrived, terms, terms_in, sums, sums_in, delta, returned, up_ref,
    w_sem, d_send, d_recv, r_send, r_recv, x_send, x_recv,
):
    me = lax.axis_index("dp")
    t = lax.axis_index("tensor")
    pair = t + 1 - 2 * (t % 2)
    across = (t + 2) % 4
    targets = {0: t, 1: pair, 2: across, 3: (pair + 2) % 4}
    order = (3, 2, 1, 0)
    width = part.shape[2]
    rank = down_ref.shape[0]
    span = up_q_ref.shape[0]
    groups = back_ref.shape[0]
    members = owners // groups

    def partner(i):
        total, bit = 0, 1
        while bit < owners:
            total = total + ((me // bit + i // bit) % 2) * bit
            bit *= 2
        return total

    q_width = wq_ref.shape[1] // 4
    kv_width = wk_ref.shape[1] // 4

    def turn(j):
        return (j + owners // 2 - 2) % (owners - 1) + 1

    def weight_copies(k):
        q_cols = pl.ds(pl.multiple_of(targets[k] * q_width, 128), q_width)
        kv_cols = pl.ds(pl.multiple_of(targets[k] * kv_width, 128), kv_width)
        return (
            pltpu.make_async_copy(
                wq_ref.at[:, q_cols], wbuf.at[k, :, pl.ds(0, q_width)], w_sem.at[k, 0]
            ),
            pltpu.make_async_copy(
                wk_ref.at[:, kv_cols], wbuf.at[k, :, pl.ds(q_width, kv_width)], w_sem.at[k, 1]
            ),
            pltpu.make_async_copy(
                wv_ref.at[:, kv_cols],
                wbuf.at[k, :, pl.ds(q_width + kv_width, kv_width)],
                w_sem.at[k, 2],
            ),
        )

    for k in order:
        for copy in weight_copies(k):
            copy.start()

    barrier = pltpu.get_barrier_semaphore()

    @pl.loop(1, owners)
    def _(i):
        pl.semaphore_signal(
            barrier, inc=1, device_id={"dp": partner(i)}, device_id_type=MESH
        )

    for peer in (pair, across):
        pl.semaphore_signal(barrier, inc=1, device_id={"tensor": peer}, device_id_type=MESH)
    pl.semaphore_wait(barrier, owners + 1)

    def dispatch_copy(i):
        return pltpu.make_async_remote_copy(
            src_ref=outgoing.at[i],
            dst_ref=arrived.at[i],
            send_sem=d_send.at[i],
            recv_sem=d_recv.at[i],
            device_id={"dp": partner(i)},
            device_id_type=MESH,
        )

    def return_copy(i):
        return pltpu.make_async_remote_copy(
            src_ref=delta.at[i],
            dst_ref=returned.at[i],
            send_sem=r_send.at[i],
            recv_sem=r_recv.at[i],
            device_id={"dp": partner(i)},
            device_id_type=MESH,
        )

    def tensor_copy(src, dst, number, peer):
        return pltpu.make_async_remote_copy(
            src_ref=src,
            dst_ref=dst,
            send_sem=x_send.at[number],
            recv_sem=x_recv.at[number],
            device_id={"tensor": peer},
            device_id_type=MESH,
        )

    def picked(i):
        return jnp.dot(
            disp_ref[i], hid_ref[...], preferred_element_type=jnp.float32
        ).astype(jnp.bfloat16)

    @pl.loop(1, owners)
    def _(j):
        i = turn(j)
        outgoing[i] = picked(i)
        dispatch_copy(i).start()

    arrived[0] = picked(0)

    tile = 256

    def project(k):
        for copy in weight_copies(k):
            copy.wait()

        @pl.loop(0, width // tile)
        def _(c):
            cols = pl.ds(pl.multiple_of(c * tile, tile), tile)
            part[k, :, cols] = jnp.dot(
                hid_ref[...], wbuf[k, :, cols], preferred_element_type=jnp.float32
            )

    own_copy = tensor_copy(part.at[1], rs1.at[0], 0, pair)
    far_copy = tensor_copy(part.at[3], rs1.at[1], 1, pair)
    sum_copy = tensor_copy(part.at[2], rs2, 2, across)
    project(3)
    far_copy.start()
    project(2)
    far_copy.wait()
    part[2] = part[2] + rs1[1]
    sum_copy.start()
    project(1)
    own_copy.start()
    project(0)

    own_copy.wait()
    part[0] = part[0] + rs1[0]
    terms[...] = jnp.zeros_like(terms)
    up_ref[...] = jnp.zeros_like(up_ref)
    up_ref[pl.ds(0, span), pl.ds(0, q_width)] = up_q_ref[...]
    up_ref[pl.ds(span, span), pl.ds(q_width, kv_width)] = up_kv_ref[0]
    up_ref[pl.ds(2 * span, span), pl.ds(q_width + kv_width, kv_width)] = up_kv_ref[1]

    def pair_copy(i):
        return tensor_copy(terms.at[i], terms_in.at[i], 3 + i, pair)

    def across_copy(i):
        return tensor_copy(sums.at[i], sums_in.at[i], 3 + owners + i, across)

    def expand(i):
        shrunk = (sums[i] + sums_in[i])[:, :rank].astype(jnp.bfloat16)
        return jnp.dot(
            shrunk, up_ref[...], preferred_element_type=jnp.float32
        ).astype(jnp.bfloat16)

    def shrink(i):
        terms[i, :, pl.ds(0, rank)] = lax.dot_general(
            arrived[i],
            down_ref[...],
            (((1,), (1,)), ((), ())),
            preferred_element_type=jnp.float32,
        )
        pair_copy(i).start()

    def reduce_pair(i):
        pair_copy(i).wait()
        sums[i] = terms[i] + terms_in[i]
        across_copy(i).start()

    shrink(0)
    reduce_pair(0)
    across_copy(0).wait()
    returned[0] = expand(0)

    @pl.loop(1, owners + 2)
    def _(j):
        @pl.when(j < owners)
        def _():
            dispatch_copy(turn(j)).wait()
            shrink(turn(j))

        @pl.when((j >= 2) & (j <= owners))
        def _():
            reduce_pair(turn(j - 1))

        @pl.when(j >= 3)
        def _():
            i = turn(j - 2)
            across_copy(i).wait()
            delta[i] = expand(i)
            return_copy(i).start()

    sum_copy.wait()
    part[0] = part[0] + rs2[...]
    part[1] = jnp.zeros(part.shape[1:], jnp.float32)

    @pl.loop(0, groups)
    def _(count):
        g = groups - 1 - count

        @pl.loop(0, members)
        def _(j):
            @pl.when(g * members + j > 0)
            def _():
                return_copy(g * members + j).wait()

        if members == 1:
            block = returned[g]
        else:
            block = returned[pl.ds(g * members, members)]
            block = block.reshape(members * block.shape[1], width)
        part[1] = part[1] + jnp.dot(back_ref[g], block, preferred_element_type=jnp.float32)

    out_ref[...] = (part[0] + adapter_scale * part[1]).astype(jnp.bfloat16)


def shards(
    hidden,
    query_weight,
    key_weight,
    value_weight,
    adapter_down_weight,
    adapter_up_query,
    adapter_up_key_value,
    cached_keys,
    cached_values,
    adapter_index,
    cache_length,
):
    step_count, request_count, part_width = hidden.shape
    row_count = step_count * request_count
    flat_rows = hidden.reshape(row_count, part_width)
    owners = lax.axis_size("dp")
    rank_span = adapter_up_query.shape[1]
    query_width = adapter_up_query.shape[2]
    kv_width = adapter_up_key_value.shape[3]
    width = query_width + 2 * kv_width
    rank_pad = -(-3 * rank_span // 128) * 128
    capacity = max(2, 2 * request_count // owners)
    slot_rows = capacity * step_count
    chosen = adapter_index[:, 0]
    places = jnp.arange(request_count, dtype=jnp.int32)
    earlier = (chosen[:, None] == chosen[None, :]) & (places[None, :] < places[:, None])
    order = jnp.sum(earlier.astype(jnp.int32), axis=1)
    offset = chosen ^ lax.axis_index("dp")
    steps = jnp.arange(step_count, dtype=jnp.int32)
    slot = (offset * slot_rows + order)[None, :] + capacity * steps[:, None]
    slot = slot.reshape(row_count)
    numbers = jnp.arange(owners * slot_rows, dtype=jnp.int32)
    dispatch = (numbers.reshape(owners, slot_rows, 1) == slot[None, None, :]).astype(jnp.bfloat16)
    groups = 2 if slot_rows % 16 == 0 and owners * slot_rows % 256 == 0 else owners
    back = (numbers.reshape(groups, 1, -1) == slot[None, :, None]).astype(jnp.bfloat16)
    down = adapter_down_weight[0].T
    f32, bf16 = jnp.float32, jnp.bfloat16
    vmem = pl.BlockSpec(memory_space=pltpu.VMEM)
    hbm = pl.BlockSpec(memory_space=pl.ANY)
    rows = pl.pallas_call(
        functools.partial(project_kernel, owners),
        out_shape=jax.ShapeDtypeStruct((row_count, width), bf16),
        in_specs=[vmem] * 6 + [hbm] * 3,
        out_specs=vmem,
        scratch_shapes=[
            pltpu.VMEM((4, part_width, width), bf16),
            pltpu.VMEM((4, row_count, width), f32),
            pltpu.VMEM((2, row_count, width), f32),
            pltpu.VMEM((row_count, width), f32),
            pltpu.VMEM((owners, slot_rows, part_width), bf16),
            pltpu.VMEM((owners, slot_rows, part_width), bf16),
            pltpu.VMEM((owners, slot_rows, rank_pad), f32),
            pltpu.VMEM((owners, slot_rows, rank_pad), f32),
            pltpu.VMEM((owners, slot_rows, rank_pad), f32),
            pltpu.VMEM((owners, slot_rows, rank_pad), f32),
            pltpu.VMEM((owners, slot_rows, width), bf16),
            pltpu.VMEM((owners, slot_rows, width), bf16),
            pltpu.VMEM((3 * rank_span, width), bf16),
            pltpu.SemaphoreType.DMA((4, 3)),
            pltpu.SemaphoreType.DMA((owners,)),
            pltpu.SemaphoreType.DMA((owners,)),
            pltpu.SemaphoreType.DMA((owners,)),
            pltpu.SemaphoreType.DMA((owners,)),
            pltpu.SemaphoreType.DMA((3 + 2 * owners,)),
            pltpu.SemaphoreType.DMA((3 + 2 * owners,)),
        ],
        compiler_params=pltpu.CompilerParams(
            collective_id=0, has_side_effects=True, vmem_limit_bytes=52 * 1024 * 1024
        ),
    )(flat_rows, dispatch, back, down, adapter_up_query[0], adapter_up_key_value[0], query_weight, key_weight, value_weight)
    query_rows = rows[:, :query_width]
    appended_keys = rows[:, query_width : query_width + kv_width]
    appended_values = rows[:, query_width + kv_width :]
    local_heads = query_width // HEAD_WIDTH
    local_kv = kv_width // HEAD_WIDTH
    group_width = local_heads // local_kv
    cache_depth = cached_keys.shape[1]
    head_rows = query_rows.reshape(step_count, request_count, local_kv, group_width, HEAD_WIDTH)
    fresh_keys = appended_keys.reshape(step_count, request_count, local_kv, HEAD_WIDTH)
    fresh_values = appended_values.reshape(step_count, request_count, local_kv, HEAD_WIDTH)
    prior_keys = cached_keys.reshape(request_count, cache_depth, local_kv, HEAD_WIDTH)
    prior_values = cached_values.reshape(request_count, cache_depth, local_kv, HEAD_WIDTH)
    factor = HEAD_WIDTH ** (-0.5)
    scores_old = (
        jnp.einsum("srkgd,rckd->srkgc", head_rows, prior_keys, preferred_element_type=jnp.float32)
        * factor
    )
    scores_new = (
        jnp.einsum("srkgd,trkd->srkgt", head_rows, fresh_keys, preferred_element_type=jnp.float32)
        * factor
    )
    valid_old = jnp.arange(cache_depth, dtype=jnp.int32)[None, :] < cache_length[:, None]
    valid_new = (
        jnp.arange(step_count, dtype=jnp.int32)[None, :]
        <= jnp.arange(step_count, dtype=jnp.int32)[:, None]
    )
    scores_old = jnp.where(valid_old[None, :, None, None, :], scores_old, -1e30)
    scores_new = jnp.where(valid_new[:, None, None, None, :], scores_new, -1e30)
    highest = jnp.maximum(jnp.max(scores_old, axis=-1), jnp.max(scores_new, axis=-1))
    exp_old = jnp.exp(scores_old - highest[..., None])
    exp_new = jnp.exp(scores_new - highest[..., None])
    denominator = jnp.sum(exp_old, axis=-1) + jnp.sum(exp_new, axis=-1)
    weight_old = (exp_old / denominator[..., None]).astype(jnp.bfloat16)
    weight_new = (exp_new / denominator[..., None]).astype(jnp.bfloat16)
    mixed = jnp.einsum(
        "srkgc,rckd->srkgd", weight_old, prior_values, preferred_element_type=jnp.float32
    )
    mixed = mixed + jnp.einsum(
        "srkgt,trkd->srkgd", weight_new, fresh_values, preferred_element_type=jnp.float32
    )
    return mixed.reshape(step_count, request_count, query_width).astype(jnp.bfloat16)


def solution(mesh):
    return jax.shard_map(
        shards,
        mesh=mesh,
        in_specs=(
            P(None, "dp", "tensor"),
            P("tensor", None),
            P("tensor", None),
            P("tensor", None),
            P("dp", "tensor", None),
            P("dp", None, "tensor"),
            P("dp", None, None, "tensor"),
            P("dp", None, "tensor"),
            P("dp", None, "tensor"),
            P("dp", None),
            P("dp"),
        ),
        out_specs=P(None, "dp", "tensor"),
        check_vma=False,
    )
```

```python
import functools

import jax
import jax.numpy as jnp
from jax import lax
from jax.experimental import pallas as pl
from jax.experimental.pallas import tpu as pltpu
from jax.sharding import PartitionSpec as P

HEAD_WIDTH = 128
MESH = pl.DeviceIdType.MESH

adapter_scale = 0.5


def project_kernel(
    owners,
    hid_hbm, disp_ref, back_ref, down_hbm, up_q_hbm, up_kv_hbm, wq_ref, wk_ref, wv_ref,
    out_ref,
    wbuf, part, rs1, rs2, outgoing, arrived, terms, terms_in, sums, sums_in, delta, returned, up_ref,
    hid_ref, down_ref, up_q_ref, up_kv_ref, l_sem,
    w_sem, d_send, d_recv, r_send, r_recv, x_send, x_recv,
):
    me = lax.axis_index("dp")
    t = lax.axis_index("tensor")
    pair = t + 1 - 2 * (t % 2)
    across = (t + 2) % 4
    targets = {0: t, 1: pair, 2: across, 3: (pair + 2) % 4}
    order = (3, 2, 1, 0)
    width = part.shape[2]
    rank = down_ref.shape[0]
    span = up_q_ref.shape[0]
    groups = back_ref.shape[0]
    members = owners // groups

    def partner(i):
        total, bit = 0, 1
        while bit < owners:
            total = total + ((me // bit + i // bit) % 2) * bit
            bit *= 2
        return total

    q_width = wq_ref.shape[1] // 4
    kv_width = wk_ref.shape[1] // 4

    def turn(j):
        return (j + owners // 2 - 2) % (owners - 1) + 1

    def weight_copies(k):
        q_cols = pl.ds(pl.multiple_of(targets[k] * q_width, 128), q_width)
        kv_cols = pl.ds(pl.multiple_of(targets[k] * kv_width, 128), kv_width)
        return (
            pltpu.make_async_copy(
                wq_ref.at[:, q_cols], wbuf.at[k, :, pl.ds(0, q_width)], w_sem.at[k, 0]
            ),
            pltpu.make_async_copy(
                wk_ref.at[:, kv_cols], wbuf.at[k, :, pl.ds(q_width, kv_width)], w_sem.at[k, 1]
            ),
            pltpu.make_async_copy(
                wv_ref.at[:, kv_cols],
                wbuf.at[k, :, pl.ds(q_width + kv_width, kv_width)],
                w_sem.at[k, 2],
            ),
        )

    local_copies = [
        pltpu.make_async_copy(hid_hbm, hid_ref, l_sem.at[0]),
        pltpu.make_async_copy(down_hbm, down_ref, l_sem.at[1]),
        pltpu.make_async_copy(up_q_hbm, up_q_ref, l_sem.at[2]),
        pltpu.make_async_copy(up_kv_hbm, up_kv_ref, l_sem.at[3]),
    ]
    local_copies[0].start()
    for k in order:
        for copy in weight_copies(k):
            copy.start()
    for copy in local_copies[1:]:
        copy.start()

    barrier = pltpu.get_barrier_semaphore()

    @pl.loop(1, owners)
    def _(i):
        pl.semaphore_signal(
            barrier, inc=1, device_id={"dp": partner(i)}, device_id_type=MESH
        )

    for peer in (pair, across):
        pl.semaphore_signal(barrier, inc=1, device_id={"tensor": peer}, device_id_type=MESH)
    local_copies[0].wait()
    pl.semaphore_wait(barrier, owners + 1)

    def dispatch_copy(i):
        return pltpu.make_async_remote_copy(
            src_ref=outgoing.at[i],
            dst_ref=arrived.at[i],
            send_sem=d_send.at[i],
            recv_sem=d_recv.at[i],
            device_id={"dp": partner(i)},
            device_id_type=MESH,
        )

    def return_copy(i):
        return pltpu.make_async_remote_copy(
            src_ref=delta.at[i],
            dst_ref=returned.at[i],
            send_sem=r_send.at[i],
            recv_sem=r_recv.at[i],
            device_id={"dp": partner(i)},
            device_id_type=MESH,
        )

    def tensor_copy(src, dst, number, peer):
        return pltpu.make_async_remote_copy(
            src_ref=src,
            dst_ref=dst,
            send_sem=x_send.at[number],
            recv_sem=x_recv.at[number],
            device_id={"tensor": peer},
            device_id_type=MESH,
        )

    def picked(i):
        return jnp.dot(
            disp_ref[i], hid_ref[...], preferred_element_type=jnp.float32
        ).astype(jnp.bfloat16)

    @pl.loop(1, owners)
    def _(j):
        i = turn(j)
        outgoing[i] = picked(i)
        dispatch_copy(i).start()

    arrived[0] = picked(0)

    tile = 256

    def project(k):
        for copy in weight_copies(k):
            copy.wait()

        @pl.loop(0, width // tile)
        def _(c):
            cols = pl.ds(pl.multiple_of(c * tile, tile), tile)
            part[k, :, cols] = jnp.dot(
                hid_ref[...], wbuf[k, :, cols], preferred_element_type=jnp.float32
            )

    own_copy = tensor_copy(part.at[1], rs1.at[0], 0, pair)
    far_copy = tensor_copy(part.at[3], rs1.at[1], 1, pair)
    sum_copy = tensor_copy(part.at[2], rs2, 2, across)
    project(3)
    far_copy.start()
    project(2)
    far_copy.wait()
    part[2] = part[2] + rs1[1]
    sum_copy.start()
    project(1)
    own_copy.start()
    project(0)

    own_copy.wait()
    part[0] = part[0] + rs1[0]
    terms[...] = jnp.zeros_like(terms)
    up_ref[...] = jnp.zeros_like(up_ref)
    for copy in local_copies[1:]:
        copy.wait()
    up_ref[pl.ds(0, span), pl.ds(0, q_width)] = up_q_ref[...]
    up_ref[pl.ds(span, span), pl.ds(q_width, kv_width)] = up_kv_ref[0]
    up_ref[pl.ds(2 * span, span), pl.ds(q_width + kv_width, kv_width)] = up_kv_ref[1]

    def pair_copy(i):
        return tensor_copy(terms.at[i], terms_in.at[i], 3 + i, pair)

    def across_copy(i):
        return tensor_copy(sums.at[i], sums_in.at[i], 3 + owners + i, across)

    def expand(i):
        shrunk = (sums[i] + sums_in[i])[:, :rank].astype(jnp.bfloat16)
        return jnp.dot(
            shrunk, up_ref[...], preferred_element_type=jnp.float32
        ).astype(jnp.bfloat16)

    def shrink(i):
        terms[i, :, pl.ds(0, rank)] = lax.dot_general(
            arrived[i],
            down_ref[...],
            (((1,), (1,)), ((), ())),
            preferred_element_type=jnp.float32,
        )
        pair_copy(i).start()

    def reduce_pair(i):
        pair_copy(i).wait()
        sums[i] = terms[i] + terms_in[i]
        across_copy(i).start()

    shrink(0)
    reduce_pair(0)
    across_copy(0).wait()
    returned[0] = expand(0)

    @pl.loop(1, owners + 2)
    def _(j):
        @pl.when(j < owners)
        def _():
            dispatch_copy(turn(j)).wait()
            shrink(turn(j))

        @pl.when((j >= 2) & (j <= owners))
        def _():
            reduce_pair(turn(j - 1))

        @pl.when(j >= 3)
        def _():
            i = turn(j - 2)
            across_copy(i).wait()
            delta[i] = expand(i)
            return_copy(i).start()

    sum_copy.wait()
    part[0] = part[0] + rs2[...]
    part[1] = jnp.zeros(part.shape[1:], jnp.float32)

    @pl.loop(0, groups)
    def _(count):
        g = groups - 1 - count

        @pl.loop(0, members)
        def _(j):
            @pl.when(g * members + j > 0)
            def _():
                return_copy(g * members + j).wait()

        if members == 1:
            block = returned[g]
        else:
            block = returned[pl.ds(g * members, members)]
            block = block.reshape(members * block.shape[1], width)
        part[1] = part[1] + jnp.dot(back_ref[g], block, preferred_element_type=jnp.float32)

    out_ref[...] = (part[0] + adapter_scale * part[1]).astype(jnp.bfloat16)


def shards(
    hidden,
    query_weight,
    key_weight,
    value_weight,
    adapter_down_weight,
    adapter_up_query,
    adapter_up_key_value,
    cached_keys,
    cached_values,
    adapter_index,
    cache_length,
):
    step_count, request_count, part_width = hidden.shape
    row_count = step_count * request_count
    flat_rows = hidden.reshape(row_count, part_width)
    owners = lax.axis_size("dp")
    rank_span = adapter_up_query.shape[1]
    query_width = adapter_up_query.shape[2]
    kv_width = adapter_up_key_value.shape[3]
    width = query_width + 2 * kv_width
    rank_pad = -(-3 * rank_span // 128) * 128
    capacity = max(2, 2 * request_count // owners)
    slot_rows = capacity * step_count
    chosen = adapter_index[:, 0]
    places = jnp.arange(request_count, dtype=jnp.int32)
    earlier = (chosen[:, None] == chosen[None, :]) & (places[None, :] < places[:, None])
    order = jnp.sum(earlier.astype(jnp.int32), axis=1)
    offset = chosen ^ lax.axis_index("dp")
    steps = jnp.arange(step_count, dtype=jnp.int32)
    slot = (offset * slot_rows + order)[None, :] + capacity * steps[:, None]
    slot = slot.reshape(row_count)
    numbers = jnp.arange(owners * slot_rows, dtype=jnp.int32)
    dispatch = (numbers.reshape(owners, slot_rows, 1) == slot[None, None, :]).astype(jnp.bfloat16)
    groups = 2 if slot_rows % 16 == 0 and owners * slot_rows % 256 == 0 else owners
    back = (numbers.reshape(groups, 1, -1) == slot[None, :, None]).astype(jnp.bfloat16)
    down = adapter_down_weight[0].T
    f32, bf16 = jnp.float32, jnp.bfloat16
    vmem = pl.BlockSpec(memory_space=pltpu.VMEM)
    hbm = pl.BlockSpec(memory_space=pltpu.HBM)
    rows = pl.pallas_call(
        functools.partial(project_kernel, owners),
        out_shape=jax.ShapeDtypeStruct((row_count, width), bf16),
        in_specs=[hbm] + [vmem] * 2 + [hbm] * 6,
        out_specs=vmem,
        scratch_shapes=[
            pltpu.VMEM((4, part_width, width), bf16),
            pltpu.VMEM((4, row_count, width), f32),
            pltpu.VMEM((2, row_count, width), f32),
            pltpu.VMEM((row_count, width), f32),
            pltpu.VMEM((owners, slot_rows, part_width), bf16),
            pltpu.VMEM((owners, slot_rows, part_width), bf16),
            pltpu.VMEM((owners, slot_rows, rank_pad), f32),
            pltpu.VMEM((owners, slot_rows, rank_pad), f32),
            pltpu.VMEM((owners, slot_rows, rank_pad), f32),
            pltpu.VMEM((owners, slot_rows, rank_pad), f32),
            pltpu.VMEM((owners, slot_rows, width), bf16),
            pltpu.VMEM((owners, slot_rows, width), bf16),
            pltpu.VMEM((3 * rank_span, width), bf16),
            pltpu.VMEM((row_count, part_width), bf16),
            pltpu.VMEM((3 * rank_span, part_width), bf16),
            pltpu.VMEM((rank_span, query_width), bf16),
            pltpu.VMEM((2, rank_span, kv_width), bf16),
            pltpu.SemaphoreType.DMA((4,)),
            pltpu.SemaphoreType.DMA((4, 3)),
            pltpu.SemaphoreType.DMA((owners,)),
            pltpu.SemaphoreType.DMA((owners,)),
            pltpu.SemaphoreType.DMA((owners,)),
            pltpu.SemaphoreType.DMA((owners,)),
            pltpu.SemaphoreType.DMA((3 + 2 * owners,)),
            pltpu.SemaphoreType.DMA((3 + 2 * owners,)),
        ],
        compiler_params=pltpu.CompilerParams(
            collective_id=0, has_side_effects=True, vmem_limit_bytes=63 * 1024 * 1024
        ),
    )(flat_rows, dispatch, back, down, adapter_up_query[0], adapter_up_key_value[0], query_weight, key_weight, value_weight)
    query_rows = rows[:, :query_width]
    appended_keys = rows[:, query_width : query_width + kv_width]
    appended_values = rows[:, query_width + kv_width :]
    local_heads = query_width // HEAD_WIDTH
    local_kv = kv_width // HEAD_WIDTH
    group_width = local_heads // local_kv
    cache_depth = cached_keys.shape[1]
    head_rows = query_rows.reshape(step_count, request_count, local_kv, group_width, HEAD_WIDTH)
    fresh_keys = appended_keys.reshape(step_count, request_count, local_kv, HEAD_WIDTH)
    fresh_values = appended_values.reshape(step_count, request_count, local_kv, HEAD_WIDTH)
    prior_keys = cached_keys.reshape(request_count, cache_depth, local_kv, HEAD_WIDTH)
    prior_values = cached_values.reshape(request_count, cache_depth, local_kv, HEAD_WIDTH)
    factor = HEAD_WIDTH ** (-0.5)
    scores_old = (
        jnp.einsum("srkgd,rckd->srkgc", head_rows, prior_keys, preferred_element_type=jnp.float32)
        * factor
    )
    scores_new = (
        jnp.einsum("srkgd,trkd->srkgt", head_rows, fresh_keys, preferred_element_type=jnp.float32)
        * factor
    )
    valid_old = jnp.arange(cache_depth, dtype=jnp.int32)[None, :] < cache_length[:, None]
    valid_new = (
        jnp.arange(step_count, dtype=jnp.int32)[None, :]
        <= jnp.arange(step_count, dtype=jnp.int32)[:, None]
    )
    scores_old = jnp.where(valid_old[None, :, None, None, :], scores_old, -1e30)
    scores_new = jnp.where(valid_new[:, None, None, None, :], scores_new, -1e30)
    highest = jnp.maximum(jnp.max(scores_old, axis=-1), jnp.max(scores_new, axis=-1))
    exp_old = jnp.exp(scores_old - highest[..., None])
    exp_new = jnp.exp(scores_new - highest[..., None])
    denominator = jnp.sum(exp_old, axis=-1) + jnp.sum(exp_new, axis=-1)
    weight_old = (exp_old / denominator[..., None]).astype(jnp.bfloat16)
    weight_new = (exp_new / denominator[..., None]).astype(jnp.bfloat16)
    mixed = jnp.einsum(
        "srkgc,rckd->srkgd", weight_old, prior_values, preferred_element_type=jnp.float32
    )
    mixed = mixed + jnp.einsum(
        "srkgt,trkd->srkgd", weight_new, fresh_values, preferred_element_type=jnp.float32
    )
    return mixed.reshape(step_count, request_count, query_width).astype(jnp.bfloat16)


def solution(mesh):
    return jax.shard_map(
        shards,
        mesh=mesh,
        in_specs=(
            P(None, "dp", "tensor"),
            P("tensor", None),
            P("tensor", None),
            P("tensor", None),
            P("dp", "tensor", None),
            P("dp", None, "tensor"),
            P("dp", None, None, "tensor"),
            P("dp", None, "tensor"),
            P("dp", None, "tensor"),
            P("dp", None),
            P("dp"),
        ),
        out_specs=P(None, "dp", "tensor"),
        check_vma=False,
    )
```
